32 devices in a mesh: groups: 2 (over x), seq: 8 (over z, y), heads: 2 (over core).
Axes of the slice: x: 2, y: 2, z: 4, core: 2. Of those that a mesh axis runs over, the one named last changes fastest.
Arguments:
- x_in: bfloat16 [2048, 8192], P(('groups', 'seq'), 'heads'), parts along dimension 0, may hold values from -6 to 6
- z_in: bfloat16 [2048, 8192], P(('groups', 'seq'), 'heads'), parts along dimension 0, may hold values from -6 to 6
- bc_in: bfloat16 [2048, 2, 512], P(('groups', 'seq'), None, 'heads'), parts along dimension 0, may hold values from -1.25 to 1.25
- conv_x_weight: bfloat16 [4, 8192], P(None, 'heads'), may hold values from -3 to 3
- conv_x_bias: float32 [8192], P('heads'), may hold values from -3 to 3
- conv_bc_weight: bfloat16 [4, 2, 512], P(None, None, 'heads'), may hold values from -3 to 3
- conv_bc_bias: float32 [2, 512], P(None, 'heads'), may hold values from -0.625 to 0.625
- dt_raw: bfloat16 [2048, 128], P(('groups', 'seq'), 'heads'), parts along dimension 0, may hold values from -3 to 3
- dt_bias: float32 [128], P('heads'), may hold values from -1 to 0.5
- decay: float32 [128], P('heads'), may hold values from 1.953125e-05 to 0.05
- skip_d: float32 [128], P('heads'), may hold values from 0.5 to 1.5
- norm_gain: float32 [8192], P('heads'), may hold values from 0.1 to 1.9
- lengths: int32 [16], P('groups'), parts along dimension 0, may hold values from 1 to 512, 1024 in all
Outputs:
- mixed: bfloat16 [2048, 8192], P(('groups', 'seq'), 'heads'), parts along dimension 0
The draws below stay inside these ranges and needn't reach their ends.
There are 2 independent parts, one for each index of `groups`. The reference program is written for one: setup_inputs(seed, part) draws one part's arguments, and reference() takes and returns one part's arrays. A program takes and returns all parts, laid end to end along the dimension named above; an argument that names none is the same for every part. Nothing has to cross between parts.
Inputs may be any that keep to these rules, and one draw needn't show every extreme that they name: `lengths`: 8 token counts that sum to 1024; the longest rollout has exactly 512 tokens.
All inputs are finite; a program needn't handle non-finite values.
Results may differ from the reference program's by a relative error of at most 0.0098.
Values may be sent and summed in bfloat16 or wider, within the bound.
A program may use at most 192 MiB of HBM per device.

```python
import math
import jax
import jax.numpy as jnp
import numpy as np
from jax import lax

HEADS = 128
HEAD_DIM = 64
STATE = 128
GROUPS = 4
KW = 4
BLOCK = 128
NSEG = 8
LENGTH = 1024
CHAN = 8192


def levels(rng, shape, shards, least, high):
    def one(dim, blocks):
        draws = jax.random.uniform(jax.random.fold_in(jax.random.fold_in(rng, 6), dim), (blocks,), jnp.float32, least / len(shards), high / len(shards))
        return jnp.repeat(jnp.exp(draws), shape[dim] // blocks).reshape((-1,) + (1,) * (len(shape) - dim - 1))

    factor_of = one(*shards[0])
    for cut in shards[1:]:
        factor_of = factor_of * one(*cut)
    return factor_of


def profile(number_of, total, bound, lean):
    portions = [(1 << 20) // math.isqrt(grade ** lean) + 1 for grade in range(2, number_of + 1)]
    rest, holding = total - bound - (number_of - 1), [1] * (number_of - 1)
    while rest > 0:
        movable = [i for i in range(number_of - 1) if holding[i] < bound]
        whole, budget = sum([portions[i] for i in movable]), rest
        for i in movable:
            addition = min(bound - holding[i], max(1, budget * portions[i] // whole), rest)
            holding[i] = holding[i] + addition
            rest = rest - addition
    return np.array([bound] + holding)


def ragged(key, count, total, bound, slope):
    if count == 2:
        one = jax.random.randint(key, (), max(1, total - bound), min(bound, total - 1) + 1)
        return jnp.stack([one, total - one])
    sizes = jnp.asarray(profile(count, total, bound, slope), jnp.int32)
    pairs = (count - 1) // 2
    donor, receiver = sizes[1:1 + 2 * pairs:2], sizes[2:2 + 2 * pairs:2]
    room = jnp.minimum(donor - 1, bound - receiver)
    shifted = jax.random.randint(jax.random.fold_in(key, 1), (pairs,), 0, 1 << 20) % (room + 1)
    sizes = sizes.at[1:1 + 2 * pairs:2].set(donor - shifted).at[2:2 + 2 * pairs:2].set(receiver + shifted)
    return sizes[jax.random.permutation(jax.random.fold_in(key, 2), count)]


def bell_draw(rng, shape, spread, bound, cuts=(), held_as=jnp.bfloat16):
    result = jax.random.normal(rng, shape, jnp.float32) * spread
    if len(cuts) > 0:
        result = levels(rng, shape, cuts, -0.22, 0.18) * result
    return jnp.clip(result, min=-bound, max=bound).astype(held_as)


def setup_inputs(seed: int = 0, part: int = 0) -> dict:
    arg_keys = jax.random.split(jax.random.key(seed), 14)
    part_splits = jax.random.split(jax.random.fold_in(arg_keys[13], part), 14)
    x_in = bell_draw(part_splits[0], (LENGTH, CHAN), 1.0, 6.0, ((0, 8), (1, 2)))
    z_in = bell_draw(part_splits[1], (LENGTH, CHAN), 1.0, 6.0, ((0, 8), (1, 2)))
    bc_in = bell_draw(part_splits[2], (LENGTH, 2, GROUPS * STATE), 0.2, 1.25, ((0, 8), (2, 2)))
    conv_x_weight = bell_draw(arg_keys[3], (KW, CHAN), KW ** -0.5, 3.0, ((1, 2),))
    conv_x_bias = bell_draw(arg_keys[4], (CHAN,), 0.5, 3.0, ((0, 2),), jnp.float32)
    conv_bc_weight = bell_draw(arg_keys[5], (KW, 2, GROUPS * STATE), KW ** -0.5, 3.0, ((2, 2),))
    conv_bc_bias = bell_draw(arg_keys[6], (2, GROUPS * STATE), 0.1, 0.625, ((1, 2),), jnp.float32)
    dt_raw = bell_draw(part_splits[7], (LENGTH, HEADS), 0.5, 3.0, ((0, 8), (1, 2)))
    dt_bias = jnp.clip(-1.0 + 1.5 * jax.random.uniform(arg_keys[8], (HEADS,), jnp.float32) ** levels(arg_keys[8], (HEADS,), ((0, 2),), -0.2, 0.2), -1.0, 0.5)
    decay = jnp.clip(jnp.exp(math.log(0.05) - 7.8477626 * jax.random.uniform(arg_keys[9], (HEADS,), jnp.float32) ** levels(arg_keys[9], (HEADS,), ((0, 2),), -0.2, 0.2)), 1.9531249563442543e-05, 0.05)
    skip_d = jnp.clip(0.5 + 1.0 * jax.random.uniform(arg_keys[10], (HEADS,), jnp.float32) ** levels(arg_keys[10], (HEADS,), ((0, 2),), -0.2, 0.2), 0.5, 1.5)
    norm_gain = jnp.clip(1.0 + 0.18 * jax.random.normal(arg_keys[11], (CHAN,), jnp.float32), 0.1, 1.9)
    lengths = ragged(part_splits[12], NSEG, LENGTH, LENGTH // 2, 2).astype(jnp.int32)
    return dict(x_in=x_in, z_in=z_in, bc_in=bc_in, conv_x_weight=conv_x_weight, conv_x_bias=conv_x_bias, conv_bc_weight=conv_bc_weight, conv_bc_bias=conv_bc_bias, dt_raw=dt_raw, dt_bias=dt_bias, decay=decay, skip_d=skip_d, norm_gain=norm_gain, lengths=lengths)


def seg_ids(ends, pos):
    count = lax.optimization_barrier(jnp.sum((ends[None, :] <= pos[:, None]).astype(jnp.int32), axis=1))
    return jnp.where(pos >= 0, count, -1).astype(jnp.int32)

def conv_act(extended, weight, bias, keep):
    rows = keep.shape[1]
    total = bias.astype(jnp.float32)
    for k in range(weight.shape[0]):
        piece = extended[k:k + rows].astype(jnp.float32) * weight[k].astype(jnp.float32)
        flag = keep[k].reshape((rows,) + (1,) * (extended.ndim - 1))
        total = total + jnp.where(flag, piece, 0.0)
    return jax.nn.silu(total).astype(jnp.bfloat16)

def contract(form, left, right):
    return jnp.einsum(form, left.astype(jnp.float32), right.astype(jnp.float32), precision=lax.Precision.HIGHEST)

def block_terms(xs, rates, decay, bmat, cmat, seg, prev_seg, block):
    count, heads, hdim = xs.shape
    groups, state = (bmat.shape[1], bmat.shape[2])
    per = heads // groups
    blocks = count // block
    xb = xs.reshape(blocks, block, groups, per, hdim)
    rate_b = rates.reshape(blocks, block, groups, per)
    cum = jnp.cumsum(-rate_b * decay.reshape(groups, per), axis=1)
    segb = seg.reshape(blocks, block)
    bb = bmat.reshape(blocks, block, groups, state)
    cb = cmat.reshape(blocks, block, groups, state)
    scores = contract('btgn,bsgn->bgts', cb, bb)
    order = jnp.arange(block)
    mask = (segb[:, :, None] == segb[:, None, :]) & (order[:, None] >= order[None, :])
    cum_t = jnp.transpose(cum, (0, 2, 3, 1))
    diff = cum_t[..., :, None] - cum_t[..., None, :]
    mask5 = mask[:, None, None]
    decays = jnp.where(mask5, jnp.exp(jnp.where(mask5, diff, 0.0)), 0.0)
    rate_t = jnp.transpose(rate_b, (0, 2, 3, 1))
    weights = (decays * scores[:, :, None] * rate_t[..., None, :]).astype(jnp.bfloat16)
    inner = contract('bgkts,bsgkp->btgkp', weights, xb)
    last = cum[:, -1]
    same_end = segb == segb[:, -1:]
    to_end = jnp.where(same_end[:, :, None, None], jnp.exp(last[:, None] - cum), 0.0) * rate_b
    scaled = (to_end[..., None] * xb.astype(jnp.float32)).astype(jnp.bfloat16)
    states = contract('bsgn,bsgkp->bgknp', bb, scaled)
    live = segb == prev_seg[:, None]
    carry = jnp.where(live[:, -1][:, None, None], jnp.exp(last), 0.0)
    entry = jnp.where(live[:, :, None, None], jnp.exp(cum), 0.0)
    return (inner, states, carry, entry, cb, xb)

def combine(earlier, later):
    return (earlier[0] * later[0], later[0][..., None, None] * earlier[1] + later[1])

def prefix_blocks(carry, states):
    return lax.associative_scan(combine, (carry, states), axis=0)

def finish(pieces, prefix, skip, start):
    inner, states, carry, entry, cb, xb = pieces
    blocks, block, groups, per, hdim = xb.shape
    lead_g = jnp.concatenate([jnp.ones_like(prefix[0][:1]), prefix[0][:-1]], axis=0)
    lead_s = jnp.concatenate([jnp.zeros_like(prefix[1][:1]), prefix[1][:-1]], axis=0)
    entering = (lead_s + lead_g[..., None, None] * start[None]).astype(jnp.bfloat16)
    outer = contract('btgn,bgknp->btgkp', cb, entering) * entry[..., None]
    total = inner + outer + skip.reshape(groups, per)[:, :, None] * xb.astype(jnp.float32)
    return total.reshape(blocks * block, groups * per, hdim).astype(jnp.bfloat16)

def gated_norm(y, gate, gain, gsize):
    rows, width = y.shape
    mixed = y.astype(jnp.float32) * jax.nn.silu(gate.astype(jnp.float32))
    grouped = mixed.reshape(rows, width // gsize, gsize)
    meansq = lax.optimization_barrier(jnp.mean(grouped * grouped, axis=-1, keepdims=True))
    normed = (grouped * lax.rsqrt(meansq + 1e-05)).reshape(rows, width)
    return (normed * gain).astype(jnp.bfloat16)

def reference(x_in, z_in, bc_in, conv_x_weight, conv_x_bias, conv_bc_weight, conv_bc_bias, dt_raw, dt_bias, decay, skip_d, norm_gain, lengths):
    length = x_in.shape[0]
    per = HEADS // GROUPS
    ends = jnp.cumsum(lengths).astype(jnp.int32)
    position = jnp.arange(length, dtype=jnp.int32)
    own = seg_ids(ends, position)
    width = conv_x_weight.shape[0]
    keep = jnp.stack([seg_ids(ends, position - (width - 1) + k) == own for k in range(width)])
    x_ext = jnp.concatenate([jnp.zeros((width - 1,) + x_in.shape[1:], x_in.dtype), x_in], axis=0)
    bc_ext = jnp.concatenate([jnp.zeros((width - 1,) + bc_in.shape[1:], bc_in.dtype), bc_in], axis=0)
    xc = conv_act(x_ext, conv_x_weight, conv_x_bias, keep)
    bcc = conv_act(bc_ext, conv_bc_weight, conv_bc_bias, keep)
    rates = jax.nn.softplus(dt_raw.astype(jnp.float32) + dt_bias)
    prev_seg = seg_ids(ends, jnp.arange(length // BLOCK, dtype=jnp.int32) * BLOCK - 1)
    xh = xc.reshape(length, GROUPS, per, HEAD_DIM)
    bm = bcc[:, 0].reshape(length, GROUPS, STATE)
    cm = bcc[:, 1].reshape(length, GROUPS, STATE)
    rate_g = rates.reshape(length, GROUPS, per)
    decay_g = decay.reshape(GROUPS, per)
    skip_g = skip_d.reshape(GROUPS, per)

    def one_group(index):
        xs = lax.dynamic_index_in_dim(xh, index, 1, keepdims=False)
        rs = lax.dynamic_index_in_dim(rate_g, index, 1, keepdims=False)
        bsel = lax.dynamic_index_in_dim(bm, index, 1, keepdims=True)
        csel = lax.dynamic_index_in_dim(cm, index, 1, keepdims=True)
        dsel = lax.dynamic_index_in_dim(decay_g, index, 0, keepdims=False)
        ksel = lax.dynamic_index_in_dim(skip_g, index, 0, keepdims=False)
        pieces = block_terms(xs, rs, dsel, bsel, csel, own, prev_seg, BLOCK)
        prefix = prefix_blocks(pieces[2], pieces[1])
        start = jnp.zeros((1, per, STATE, HEAD_DIM), jnp.float32)
        return finish(pieces, prefix, ksel, start)
    outs = lax.map(one_group, jnp.arange(GROUPS, dtype=jnp.int32))
    y = jnp.transpose(outs, (1, 0, 2, 3)).reshape(length, HEADS * HEAD_DIM)
    return gated_norm(y, z_in, norm_gain, HEADS * HEAD_DIM // GROUPS)
```

```python
import functools

import jax
import jax.numpy as jnp
from jax import lax
from jax.experimental import pallas as pl
from jax.experimental.pallas import tpu as pltpu
from jax.sharding import PartitionSpec as P

HEAD_DIM = 64
STATE = 128
BLOCK = 128
TILE = 128
CHUNK = 256
EDGE = 16
LAG = 2
F32 = jnp.float32
BF16 = jnp.bfloat16
MESH = pl.DeviceIdType.MESH


def dot(a, b):
    return lax.dot_general(a, b, (((1,), (0,)), ((), ())), preferred_element_type=F32)


def silu(v):
    half = 0.5 * v
    return half + half * jnp.tanh(half)


def split(v):
    high = v.astype(BF16).astype(F32)
    return jnp.concatenate([high, v - high], axis=1)


def iota(shape, dim):
    return lax.broadcasted_iota(jnp.int32, shape, dim)


def spread(chunk, heads):
    per = CHUNK // HEAD_DIM
    row = iota((2 * heads, CHUNK), 0)
    col = iota((2 * heads, CHUNK), 1)
    head = jnp.where(row >= heads, row - heads, row)
    hit = head == chunk * per + lax.shift_right_logical(col, HEAD_DIM.bit_length() - 1)
    return jnp.where(hit, 1.0, 0.0).astype(BF16)


def conv_rows(values, weight, bias, flags, skip_rows):
    width = weight.shape[0]
    total = bias + values[skip_rows:] * weight[width - 1 : width]
    for d in range(1, width):
        moved = pltpu.roll(values, d, 0)[skip_rows:]
        total = total + moved * flags[d - 1] * weight[width - 1 - d : width - d]
    return silu(total).astype(BF16)


def kernel(
    peers,
    lengths,
    x_hbm,
    z_hbm,
    bc,
    wx,
    bx,
    wbc,
    bbc,
    dt,
    dtb,
    decay,
    skip,
    gain,
    out,
    xv,
    zv,
    xa,
    bca,
    xp,
    ent,
    flags,
    halo_x,
    halo_bc,
    mix,
    bt,
    grow,
    ggrow,
    vec,
    pvec,
    rows_x,
    prow,
    s_out,
    s_own,
    s_in,
    e_in,
    e_out,
    t_out,
    gated,
    sumsq,
    local_sem,
    halo_send,
    halo_recv,
    vec_send,
    vec_recv,
    s_send,
    s_recv,
    e_send,
    e_recv,
    t_send,
    t_recv,
):
    rows, chan = x_hbm.shape
    heads = dt.shape[1]
    groups = bc.shape[1] // (2 * STATE)
    chunks = chan // CHUNK
    pairs = chunks // 2
    pairs_per = pairs // groups
    me = lax.axis_index("seq")
    inner = lax.rem(me, 2)
    outer = lax.div(me, 2)
    last_outer = peers // 2 - 1
    partner = me + 1 - 2 * inner

    load_x = pltpu.make_async_copy(x_hbm, xv, local_sem.at[0])
    load_z = pltpu.make_async_copy(z_hbm, zv, local_sem.at[1])
    load_x.start()
    load_z.start()

    barrier = pltpu.get_barrier_semaphore()
    for step in (-2, -1, 1, 2):
        there = me + step

        @pl.when((there >= 0) & (there < peers))
        def _():
            pl.semaphore_signal(barrier, inc=1, device_id={"seq": there}, device_id_type=MESH)

    present = jnp.minimum(me, 2) + jnp.minimum(peers - 1 - me, 2)

    start = me * rows
    ends = []
    total = jnp.int32(0)
    for j in range(lengths.shape[0]):
        total = total + lengths[j]
        ends.append(total)

    def seg_of(pos):
        count = jnp.zeros_like(pos)
        for end in ends:
            count = count + jnp.where(pos >= end, 1, 0)
        return jnp.where(pos >= 0, count, -1)

    square = (rows, rows)
    pos = iota(square, 0) + start
    seg_t = seg_of(pos)
    for d in range(1, wx.shape[0]):
        flags[d - 1] = jnp.where(seg_of(pos - d) == seg_t, 1.0, 0.0)
    seg_s = seg_of(iota(square, 1) + start)
    seg_last = seg_of(jnp.zeros(square, jnp.int32) + (start + rows - 1))
    seg_prev = seg_of(jnp.zeros(square, jnp.int32) + (start - 1))
    mask = jnp.where((seg_t == seg_s) & (iota(square, 0) >= iota(square, 1)), 1.0, 0.0)
    to_end = jnp.where(seg_t == seg_last, 1.0, 0.0)
    live = jnp.where(seg_t == seg_prev, 1.0, 0.0)

    raw = dt[...].astype(F32) + dtb[...]
    rate = jnp.maximum(raw, 0.0) + jnp.log(1.0 + jnp.exp(-jnp.abs(raw)))
    a = -rate * decay[...]
    tri = jnp.where(iota(square, 0) >= iota(square, 1), 1.0, 0.0).astype(BF16)
    cum = jnp.zeros_like(a)
    rest = a
    for _ in range(3):
        part = rest.astype(BF16)
        cum = cum + dot(tri, part)
        rest = rest - part.astype(F32)
    grow[...] = split(jnp.exp(cum)).astype(BF16)
    ggrow[...] = split(jnp.exp(-cum) * rate).astype(BF16)
    whole = jnp.exp(cum[rows - 1 : rows, :])
    carry = live[rows - 1 : rows, :heads] * whole
    which = iota(vec.shape, 0)
    vec[...] = jnp.where(
        which == 0, split(carry), jnp.where(which == 1, split(whole), jnp.where(which == 2, split(skip[...]), 0.0))
    )

    pl.semaphore_wait(barrier, present)

    def halo_copies():
        there = jnp.minimum(me + 1, peers - 1)
        tail = pl.ds(rows - EDGE, EDGE)
        return [
            pltpu.make_async_remote_copy(
                x_hbm.at[tail], halo_x, halo_send.at[0], halo_recv.at[0], device_id={"seq": there}, device_id_type=MESH
            ),
            pltpu.make_async_remote_copy(
                bc.at[tail], halo_bc, halo_send.at[1], halo_recv.at[1], device_id={"seq": there}, device_id_type=MESH
            ),
        ]

    @pl.when(me < peers - 1)
    def _():
        for copy in halo_copies():
            copy.start()

    def vec_copy():
        return pltpu.make_async_remote_copy(
            vec, pvec, vec_send, vec_recv, device_id={"seq": partner}, device_id_type=MESH
        )

    vec_copy().start()

    for tile in range(bc.shape[1] // TILE):
        cols = slice(tile * TILE, (tile + 1) * TILE)
        bca[:, cols] = conv_rows(bc[:, cols].astype(F32), wbc[:, cols].astype(F32), bbc[:, cols], flags, 0)

    load_x.wait()

    def conv_tile(tile, _):
        cols = pl.ds(pl.multiple_of(tile * TILE, TILE), TILE)
        xa[:, cols] = conv_rows(xv[:, cols].astype(F32), wx[:, cols].astype(F32), bx[:, cols], flags, 0)
        return 0

    lax.fori_loop(0, chan // TILE, conv_tile, 0, unroll=2)

    @pl.when(me == 0)
    def _():
        halo_x[...] = jnp.zeros_like(halo_x)
        halo_bc[...] = jnp.zeros_like(halo_bc)

    @pl.when(me > 0)
    def _():
        for copy in halo_copies():
            copy.wait_recv()

    head_flags = [flags[d, :EDGE, :] for d in range(wx.shape[0] - 1)]
    for tile in range(bc.shape[1] // TILE):
        cols = slice(tile * TILE, (tile + 1) * TILE)
        values = jnp.concatenate([halo_bc[:, cols].astype(F32), bc[:EDGE, cols].astype(F32)], axis=0)
        bca[:EDGE, cols] = conv_rows(values, wbc[:, cols].astype(F32), bbc[:, cols], head_flags, EDGE)

    def conv_head(tile, _):
        cols = pl.ds(pl.multiple_of(tile * TILE, TILE), TILE)
        values = jnp.concatenate([halo_x[:, cols].astype(F32), xv[:EDGE, cols].astype(F32)], axis=0)
        some = [flags[d, :EDGE, :] for d in range(wx.shape[0] - 1)]
        xa[:EDGE, cols] = conv_rows(values, wx[:, cols].astype(F32), bx[:, cols], some, EDGE)
        return 0

    lax.fori_loop(0, chan // TILE, conv_head, 0, unroll=4)

    for g in range(groups):
        bmat = bca[:, g * STATE : (g + 1) * STATE].astype(F32)
        cmat = bca[:, (groups + g) * STATE : (groups + g + 1) * STATE]
        bmat_t = jnp.transpose(bmat)
        scores = dot(cmat, bmat_t.astype(BF16))
        mix[g, :, :rows] = (scores * mask).astype(BF16)
        mix[g, :, rows:] = (cmat.astype(F32) * live).astype(BF16)
        bt[g] = jnp.transpose(bmat * to_end).astype(BF16)

    def state_of(c):
        ex = spread(c, heads)
        cols = pl.ds(pl.multiple_of(c * CHUNK, CHUNK), CHUNK)
        scaled = (dot(ggrow[...], ex) * xa[:, cols].astype(F32)).astype(BF16)
        xp[c] = scaled
        rows_x[c] = dot(vec[...].astype(BF16), ex)
        return dot(bt[lax.div(c, chunks // groups)], scaled) * rows_x[c][1:2, :]

    def s_copy(j):
        return pltpu.make_async_remote_copy(
            s_out.at[j], s_in.at[j], s_send.at[j], s_recv.at[j], device_id={"seq": partner}, device_id_type=MESH
        )

    def e_copy(j):
        there = jnp.minimum(me + 2, peers - 1)
        return pltpu.make_async_remote_copy(
            e_out.at[j], e_in.at[j], e_send.at[j], e_recv.at[j], device_id={"seq": there}, device_id_type=MESH
        )

    def t_copy(j, c):
        return pltpu.make_async_remote_copy(
            t_out.at[j], ent.at[c], t_send.at[j], t_recv.at[j], device_id={"seq": partner}, device_id_type=MESH
        )

    def states(j, _):
        s_out[j] = state_of(2 * j + 1 - inner).astype(BF16)
        s_copy(j).start()
        s_own[j] = state_of(2 * j + inner)
        return 0

    lax.fori_loop(0, pairs, states, 0)

    @pl.when(outer == 0)
    def _():
        e_in[...] = jnp.zeros_like(e_in)

    vec_copy().wait_recv()
    pvec_b = pvec[...].astype(BF16)

    def partner_rows(j, _):
        prow[j] = dot(pvec_b, spread(2 * j + inner, heads))
        return 0

    lax.fori_loop(0, pairs, partner_rows, 0)
    sumsq[...] = jnp.zeros_like(sumsq)
    load_z.wait()

    def advance(j):
        c = 2 * j + inner
        s_copy(j).wait_recv()

        @pl.when(outer > 0)
        def _():
            e_copy(j).wait_recv()

        mine = s_own[j]
        other = s_in[j].astype(F32)
        c_mine = rows_x[c][0:1, :]
        c_other = prow[j][0:1, :]
        first = jnp.broadcast_to(inner, mine.shape) == 0
        row_first = jnp.broadcast_to(inner, c_mine.shape) == 0
        e = e_in[j].astype(F32)
        between = jnp.where(row_first, c_mine, c_other) * e + jnp.where(first, mine, other)
        after = jnp.where(row_first, c_other, c_mine) * between + jnp.where(first, other, mine)
        e_out[j] = after.astype(BF16)

        @pl.when(outer < last_outer)
        def _():
            e_copy(j).start()

        t_out[j] = jnp.where(first, between, e).astype(BF16)
        t_copy(j, c).start()
        ent[c] = jnp.where(first, e, between).astype(BF16)

    def finish_chunk(c):
        g = lax.div(c, chunks // groups)
        cols = pl.ds(pl.multiple_of(c * CHUNK, CHUNK), CHUNK)
        right = jnp.concatenate([xp[c], ent[c]], axis=0)
        y = dot(mix[g], right) * dot(grow[...], spread(c, heads))
        y = y + rows_x[c][2:3, :] * xa[:, cols].astype(F32)
        v = y.astype(BF16).astype(F32) * silu(zv[:, cols].astype(F32))
        gated[c] = v
        sumsq[g] = sumsq[g] + v * v

    def finish_pair(j):
        t_copy(j, 2 * j + 1 - inner).wait_recv()
        finish_chunk(2 * j)
        finish_chunk(2 * j + 1)

    def norm_group(g):
        size = chan // groups
        mean = jnp.sum(sumsq[g], axis=1, keepdims=True) * (1.0 / size)
        scale = lax.rsqrt(mean + 1e-05)

        def one(k, _):
            c = g * (chunks // groups) + k
            cols = pl.ds(pl.multiple_of(c * CHUNK, CHUNK), CHUNK)
            out[:, cols] = (gated[c] * scale * gain[:, cols]).astype(BF16)
            return 0

        lax.fori_loop(0, chunks // groups, one, 0, unroll=2)

    def lead(j, _):
        advance(j)
        return 0

    def steady(j, _):
        advance(j)
        finish_pair(j - LAG)

        @pl.when(lax.rem(j - LAG + 1, pairs_per) == 0)
        def _():
            norm_group(lax.div(j - LAG, pairs_per))

        return 0

    def tail(j, _):
        finish_pair(j)

        @pl.when(lax.rem(j + 1, pairs_per) == 0)
        def _():
            norm_group(lax.div(j, pairs_per))

        return 0

    lax.fori_loop(0, LAG, lead, 0)
    lax.fori_loop(LAG, pairs, steady, 0)
    lax.fori_loop(pairs - LAG, pairs, tail, 0)

    def drain(j, _):
        s_copy(j).wait_send()
        t_copy(j, 2 * j + inner).wait_send()

        @pl.when(outer < last_outer)
        def _():
            e_copy(j).wait_send()

        return 0

    lax.fori_loop(0, pairs, drain, 0)
    vec_copy().wait_send()

    @pl.when(me < peers - 1)
    def _():
        for copy in halo_copies():
            copy.wait_send()


def shards(peers, x_in, z_in, bc_in, wx, bx, wbc, bbc, dt_raw, dt_bias, decay, skip_d, gain, lengths):
    rows, chan = x_in.shape
    heads = dt_raw.shape[1]
    groups = bc_in.shape[2] // STATE
    width = wx.shape[0]
    chunks = chan // CHUNK
    pairs = chunks // 2
    bcw = 2 * groups * STATE
    vmem = pl.BlockSpec(memory_space=pltpu.VMEM)
    hbm = pl.BlockSpec(memory_space=pl.ANY)
    smem = pl.BlockSpec(memory_space=pltpu.SMEM)
    dma = pltpu.SemaphoreType.DMA
    return pl.pallas_call(
        functools.partial(kernel, peers),
        out_shape=jax.ShapeDtypeStruct((rows, chan), BF16),
        in_specs=[smem, hbm, hbm] + [vmem] * 10,
        out_specs=vmem,
        scratch_shapes=[
            pltpu.VMEM((rows, chan), BF16),
            pltpu.VMEM((rows, chan), BF16),
            pltpu.VMEM((rows, chan), BF16),
            pltpu.VMEM((rows, bcw), BF16),
            pltpu.VMEM((chunks, rows, CHUNK), BF16),
            pltpu.VMEM((chunks, STATE, CHUNK), BF16),
            pltpu.VMEM((width - 1, rows, TILE), F32),
            pltpu.VMEM((EDGE, chan), BF16),
            pltpu.VMEM((EDGE, bcw), BF16),
            pltpu.VMEM((groups, rows, rows + STATE), BF16),
            pltpu.VMEM((groups, STATE, rows), BF16),
            pltpu.VMEM((rows, 2 * heads), BF16),
            pltpu.VMEM((rows, 2 * heads), BF16),
            pltpu.VMEM((16, 2 * heads), F32),
            pltpu.VMEM((16, 2 * heads), F32),
            pltpu.VMEM((chunks, 16, CHUNK), F32),
            pltpu.VMEM((pairs, 16, CHUNK), F32),
            pltpu.VMEM((pairs, STATE, CHUNK), BF16),
            pltpu.VMEM((pairs, STATE, CHUNK), F32),
            pltpu.VMEM((pairs, STATE, CHUNK), BF16),
            pltpu.VMEM((pairs, STATE, CHUNK), BF16),
            pltpu.VMEM((pairs, STATE, CHUNK), BF16),
            pltpu.VMEM((pairs, STATE, CHUNK), BF16),
            pltpu.VMEM((chunks, rows, CHUNK), F32),
            pltpu.VMEM((groups, rows, CHUNK), F32),
            dma((2,)),
            dma((2,)),
            dma((2,)),
            dma,
            dma,
            dma((pairs,)),
            dma((pairs,)),
            dma((pairs,)),
            dma((pairs,)),
            dma((pairs,)),
            dma((pairs,)),
        ],
        compiler_params=pltpu.CompilerParams(
            collective_id=0, has_side_effects=True, vmem_limit_bytes=40 * 1024 * 1024
        ),
        name="mixer",
    )(
        lengths,
        x_in,
        z_in,
        bc_in.reshape(rows, bcw),
        wx,
        bx.reshape(1, chan),
        wbc.reshape(width, bcw),
        bbc.reshape(1, bcw),
        dt_raw,
        dt_bias.reshape(1, heads),
        decay.reshape(1, heads),
        skip_d.reshape(1, heads),
        gain.reshape(1, chan),
    )


def solution(mesh):
    return jax.shard_map(
        functools.partial(shards, mesh.shape["seq"]),
        mesh=mesh,
        in_specs=(
            P(("groups", "seq"), "heads"),
            P(("groups", "seq"), "heads"),
            P(("groups", "seq"), None, "heads"),
            P(None, "heads"),
            P("heads"),
            P(None, None, "heads"),
            P(None, "heads"),
            P(("groups", "seq"), "heads"),
            P("heads"),
            P("heads"),
            P("heads"),
            P("heads"),
            P("groups"),
        ),
        out_specs=P(("groups", "seq"), "heads"),
        check_vma=False,
    )
```

```python
import functools

import jax
import jax.numpy as jnp
from jax import lax
from jax.experimental import pallas as pl
from jax.experimental.pallas import tpu as pltpu
from jax.sharding import PartitionSpec as P

HEAD_DIM = 64
STATE = 128
BLOCK = 128
TILE = 128
CHUNK = 256
EDGE = 16
LAG = 2
EARLY = 3
FOLD = 4
F32 = jnp.float32
BF16 = jnp.bfloat16
MESH = pl.DeviceIdType.MESH


def dot(a, b):
    return lax.dot_general(a, b, (((1,), (0,)), ((), ())), preferred_element_type=F32)


def silu(v):
    half = 0.5 * v
    return half + half * jnp.tanh(half)


def split(v):
    high = v.astype(BF16).astype(F32)
    return jnp.concatenate([high, v - high], axis=1)


def iota(shape, dim):
    return lax.broadcasted_iota(jnp.int32, shape, dim)


def spread(chunk, heads):
    per = CHUNK // HEAD_DIM
    row = iota((2 * heads, CHUNK), 0)
    col = iota((2 * heads, CHUNK), 1)
    head = jnp.where(row >= heads, row - heads, row)
    hit = head == chunk * per + lax.shift_right_logical(col, HEAD_DIM.bit_length() - 1)
    return jnp.where(hit, 1.0, 0.0).astype(BF16)


def conv_rows(values, weight, bias, flags, skip_rows):
    width = weight.shape[0]
    total = bias + values[skip_rows:] * weight[width - 1 : width]
    for d in range(1, width):
        moved = pltpu.roll(values, d, 0)[skip_rows:]
        total = total + moved * flags[d - 1] * weight[width - 1 - d : width - d]
    return silu(total).astype(BF16)


def kernel(
    peers,
    lengths,
    x_hbm,
    z_hbm,
    bc,
    wx,
    bx,
    wbc,
    bbc,
    dt,
    dtb,
    decay,
    skip,
    gain,
    out,
    xv,
    zv,
    xa,
    bca,
    xp,
    ent,
    flags,
    halo_x,
    halo_bc,
    fold_out,
    fold_in,
    spreads,
    mix,
    bt,
    grow,
    ggrow,
    vec,
    pvec,
    rows_x,
    s_out,
    s_own,
    s_in,
    e_in,
    e_out,
    t_out,
    gated,
    sumsq,
    local_sem,
    halo_send,
    halo_recv,
    vec_send,
    vec_recv,
    s_send,
    s_recv,
    e_send,
    e_recv,
    t_send,
    t_recv,
):
    rows, chan = x_hbm.shape
    heads = dt.shape[1]
    groups = bc.shape[1] // (2 * STATE)
    chunks = chan // CHUNK
    pairs = chunks // 2
    pairs_per = pairs // groups
    me = lax.axis_index("seq")
    inner = lax.rem(me, 2)
    outer = lax.div(me, 2)
    last_outer = peers // 2 - 1
    partner = me + 1 - 2 * inner

    load_x = pltpu.make_async_copy(x_hbm, xv, local_sem.at[0])
    load_z = pltpu.make_async_copy(z_hbm, zv, local_sem.at[1])
    load_x.start()
    load_z.start()

    barrier = pltpu.get_barrier_semaphore()
    for step in (-2, -1, 1, 2):
        there = me + step

        @pl.when((there >= 0) & (there < peers))
        def _():
            pl.semaphore_signal(barrier, inc=1, device_id={"seq": there}, device_id_type=MESH)

    present = jnp.minimum(me, 2) + jnp.minimum(peers - 1 - me, 2)

    start = me * rows
    ends = []
    total = jnp.int32(0)
    for j in range(lengths.shape[0]):
        total = total + lengths[j]
        ends.append(total)

    def seg_of(pos):
        count = jnp.zeros_like(pos)
        for end in ends:
            count = count + jnp.where(pos >= end, 1, 0)
        return jnp.where(pos >= 0, count, -1)

    square = (rows, rows)
    pos = iota(square, 0) + start
    seg_t = seg_of(pos)
    for d in range(1, wx.shape[0]):
        flags[d - 1] = jnp.where(seg_of(pos - d) == seg_t, 1.0, 0.0)
    seg_s = seg_of(iota(square, 1) + start)
    seg_last = seg_of(jnp.zeros(square, jnp.int32) + (start + rows - 1))
    seg_prev = seg_of(jnp.zeros(square, jnp.int32) + (start - 1))
    mask = jnp.where((seg_t == seg_s) & (iota(square, 0) >= iota(square, 1)), 1.0, 0.0)
    to_end = jnp.where(seg_t == seg_last, 1.0, 0.0)
    live = jnp.where(seg_t == seg_prev, 1.0, 0.0)

    raw = dt[...].astype(F32) + dtb[...]
    rate = jnp.maximum(raw, 0.0) + jnp.log(1.0 + jnp.exp(-jnp.abs(raw)))
    a = -rate * decay[...]
    tri = jnp.where(iota(square, 0) >= iota(square, 1), 1.0, 0.0).astype(BF16)
    cum = jnp.zeros_like(a)
    rest = a
    for _ in range(3):
        part = rest.astype(BF16)
        cum = cum + dot(tri, part)
        rest = rest - part.astype(F32)
    grow[...] = split(jnp.exp(cum)).astype(BF16)
    ggrow[...] = split(jnp.exp(-cum) * rate).astype(BF16)
    whole = jnp.exp(cum[rows - 1 : rows, :])
    carry = live[rows - 1 : rows, :heads] * whole
    which = iota(vec.shape, 0)
    vec[...] = jnp.where(
        which == 0, split(carry), jnp.where(which == 1, split(whole), jnp.where(which == 2, split(skip[...]), 0.0))
    )

    load_x.wait()
    run = chan // FOLD
    quarter = lax.shift_right_logical(iota((EDGE, run), 0), 2)
    folded = jnp.zeros((EDGE, run), F32)
    for m in range(FOLD):
        piece = xv[rows - EDGE :, m * run : (m + 1) * run].astype(F32)
        moved = pltpu.roll(piece, 4 * m + 4, 0) if m < FOLD - 1 else piece
        folded = jnp.where(quarter == m, moved, folded)
    fold_out[...] = folded.astype(BF16)

    pl.semaphore_wait(barrier, present)

    def halo_copies():
        there = jnp.minimum(me + 1, peers - 1)
        tail = pl.ds(rows - EDGE, EDGE)
        return [
            pltpu.make_async_remote_copy(
                fold_out, fold_in, halo_send.at[0], halo_recv.at[0], device_id={"seq": there}, device_id_type=MESH
            ),
            pltpu.make_async_remote_copy(
                bc.at[tail], halo_bc, halo_send.at[1], halo_recv.at[1], device_id={"seq": there}, device_id_type=MESH
            ),
        ]

    @pl.when(me < peers - 1)
    def _():
        for copy in halo_copies():
            copy.start()

    def vec_copy():
        return pltpu.make_async_remote_copy(
            vec, pvec, vec_send, vec_recv, device_id={"seq": partner}, device_id_type=MESH
        )

    vec_copy().start()

    bcols = groups * STATE

    def bc_params(tile):
        cols = slice((tile % groups) * TILE, (tile % groups + 1) * TILE)
        which = tile // groups
        return wbc[:, tile * TILE : (tile + 1) * TILE].astype(F32), bbc[which : which + 1, cols]

    bc_tiles = 2 * bcols // TILE
    for tile in range(bc_tiles):
        cols = slice(tile * TILE, (tile + 1) * TILE)
        weight, bias = bc_params(tile)
        bca[:, cols] = conv_rows(bc[:, cols].astype(F32), weight, bias, flags, 0)

    def x_params(cols):
        return wx[:, cols].astype(F32), bx[:, cols]

    def conv_tile(tile, _):
        cols = pl.ds(pl.multiple_of(tile * TILE, TILE), TILE)
        weight, bias = x_params(cols)
        xa[:, cols] = conv_rows(xv[:, cols].astype(F32), weight, bias, flags, 0)
        return 0

    early_tiles = EARLY * 2 * CHUNK // TILE
    lax.fori_loop(0, early_tiles, conv_tile, 0, unroll=2)

    @pl.when(me == 0)
    def _():
        fold_in[...] = jnp.zeros_like(fold_in)
        halo_bc[...] = jnp.zeros_like(halo_bc)

    @pl.when(me > 0)
    def _():
        for copy in halo_copies():
            copy.wait_recv()

    for m in range(FOLD):
        piece = fold_in[...].astype(F32)
        moved = pltpu.roll(piece, EDGE - 4 * m - 4, 0) if m < FOLD - 1 else piece
        halo_x[:, m * run : (m + 1) * run] = moved.astype(BF16)

    head_flags = [flags[d, :EDGE, :] for d in range(wx.shape[0] - 1)]
    for tile in range(bc_tiles):
        cols = slice(tile * TILE, (tile + 1) * TILE)
        weight, bias = bc_params(tile)
        values = jnp.concatenate([halo_bc[:, cols].astype(F32), bc[:EDGE, cols].astype(F32)], axis=0)
        bca[:EDGE, cols] = conv_rows(values, weight, bias, head_flags, EDGE)

    def conv_head(tile, _):
        cols = pl.ds(pl.multiple_of(tile * TILE, TILE), TILE)
        weight, bias = x_params(cols)
        values = jnp.concatenate([halo_x[:, cols].astype(F32), xv[:EDGE, cols].astype(F32)], axis=0)
        some = [flags[d, :EDGE, :] for d in range(wx.shape[0] - 1)]
        xa[:EDGE, cols] = conv_rows(values, weight, bias, some, EDGE)
        return 0

    lax.fori_loop(0, early_tiles, conv_head, 0, unroll=2)

    def conv_whole(tile, _):
        cols = pl.ds(pl.multiple_of(tile * TILE, TILE), TILE)
        weight, bias = x_params(cols)
        values = jnp.concatenate([halo_x[:, cols].astype(F32), xv[:, cols].astype(F32)], axis=0)
        xa[:, cols] = conv_rows(values, weight, bias, flags, EDGE)
        return 0

    for g in range(groups):
        bmat = bca[:, g * STATE : (g + 1) * STATE].astype(F32)
        cmat = bca[:, (groups + g) * STATE : (groups + g + 1) * STATE]
        bmat_t = jnp.transpose(bmat)
        scores = dot(cmat, bmat_t.astype(BF16))
        mix[g, :, :rows] = (scores * mask).astype(BF16)
        mix[g, :, rows:] = (cmat.astype(F32) * live).astype(BF16)
        bt[g] = jnp.transpose(bmat * to_end).astype(BF16)

    def state_of(c):
        ex = spread(c, heads)
        spreads[c] = ex
        cols = pl.ds(pl.multiple_of(c * CHUNK, CHUNK), CHUNK)
        scaled = (dot(ggrow[...], ex) * xa[:, cols].astype(F32)).astype(BF16)
        xp[c] = scaled
        rows_x[c] = dot(vec[...].astype(BF16), ex)
        return dot(bt[lax.div(c, chunks // groups)], scaled) * rows_x[c][1:2, :]

    def s_copy(j):
        return pltpu.make_async_remote_copy(
            s_out.at[j], s_in.at[j], s_send.at[j], s_recv.at[j], device_id={"seq": partner}, device_id_type=MESH
        )

    def e_copy(j):
        there = jnp.minimum(me + 2, peers - 1)
        return pltpu.make_async_remote_copy(
            e_out.at[j], e_in.at[j], e_send.at[j], e_recv.at[j], device_id={"seq": there}, device_id_type=MESH
        )

    def t_copy(j, c):
        return pltpu.make_async_remote_copy(
            t_out.at[j], ent.at[c], t_send.at[j], t_recv.at[j], device_id={"seq": partner}, device_id_type=MESH
        )

    def advance(j):
        c = 2 * j + inner
        s_copy(j).wait_recv()

        @pl.when(outer > 0)
        def _():
            e_copy(j).wait_recv()

        mine = s_own[j]
        other = s_in[j].astype(F32)
        c_mine = rows_x[c][0:1, :]
        c_other = dot(pvec[...].astype(BF16), spreads[c])[0:1, :]
        first = jnp.broadcast_to(inner, mine.shape) == 0
        row_first = jnp.broadcast_to(inner, c_mine.shape) == 0
        e = e_in[j].astype(F32)
        between = jnp.where(row_first, c_mine, c_other) * e + jnp.where(first, mine, other)
        after = jnp.where(row_first, c_other, c_mine) * between + jnp.where(first, other, mine)
        e_out[j] = after.astype(BF16)

        @pl.when(outer < last_outer)
        def _():
            e_copy(j).start()

        t_out[j] = jnp.where(first, between, e).astype(BF16)
        t_copy(j, c).start()
        ent[c] = jnp.where(first, e, between).astype(BF16)

    @pl.when(outer == 0)
    def _():
        e_in[...] = jnp.zeros_like(e_in)

    vec_copy().wait_recv()
    sumsq[...] = jnp.zeros_like(sumsq)
    ahead = jnp.where(outer == 0, pairs - LAG, 0)

    def states(j, _):
        @pl.when(j >= EARLY)
        def _():
            per = 2 * CHUNK // TILE
            for k in range(per):
                conv_whole(j * per + k, 0)

        s_out[j] = state_of(2 * j + 1 - inner).astype(BF16)
        s_copy(j).start()
        s_own[j] = state_of(2 * j + inner)

        @pl.when((outer == 0) & (j >= LAG))
        def _():
            advance(j - LAG)

        return 0

    lax.fori_loop(0, pairs, states, 0)
    load_z.wait()

    def finish_chunk(c):
        g = lax.div(c, chunks // groups)
        cols = pl.ds(pl.multiple_of(c * CHUNK, CHUNK), CHUNK)
        right = jnp.concatenate([xp[c], ent[c]], axis=0)
        y = dot(mix[g], right) * dot(grow[...], spreads[c])
        y = y + rows_x[c][2:3, :] * xa[:, cols].astype(F32)
        v = y.astype(BF16).astype(F32) * silu(zv[:, cols].astype(F32))
        gated[c] = v
        sumsq[g] = sumsq[g] + v * v

    def finish_pair(j):
        t_copy(j, 2 * j + 1 - inner).wait_recv()
        finish_chunk(2 * j)
        finish_chunk(2 * j + 1)

    def norm_group(g):
        size = chan // groups
        mean = jnp.sum(sumsq[g], axis=1, keepdims=True) * (1.0 / size)
        scale = lax.rsqrt(mean + 1e-05)

        def one(k, _):
            c = g * (chunks // groups) + k
            cols = pl.ds(pl.multiple_of(c * CHUNK, CHUNK), CHUNK)
            out[:, cols] = (gated[c] * scale * gain[:, cols]).astype(BF16)
            return 0

        lax.fori_loop(0, chunks // groups, one, 0, unroll=2)

    def lead(j, _):
        @pl.when(j >= ahead)
        def _():
            advance(j)

        return 0

    def steady(j, _):
        @pl.when(j >= ahead)
        def _():
            advance(j)

        finish_pair(j - LAG)

        @pl.when(lax.rem(j - LAG + 1, pairs_per) == 0)
        def _():
            norm_group(lax.div(j - LAG, pairs_per))

        return 0

    def tail(j, _):
        finish_pair(j)

        @pl.when(lax.rem(j + 1, pairs_per) == 0)
        def _():
            norm_group(lax.div(j, pairs_per))

        return 0

    lax.fori_loop(0, LAG, lead, 0)
    lax.fori_loop(LAG, pairs, steady, 0)
    lax.fori_loop(pairs - LAG, pairs, tail, 0)

    def drain(j, _):
        s_copy(j).wait_send()
        t_copy(j, 2 * j + inner).wait_send()

        @pl.when(outer < last_outer)
        def _():
            e_copy(j).wait_send()

        return 0

    lax.fori_loop(0, pairs, drain, 0)
    vec_copy().wait_send()

    @pl.when(me < peers - 1)
    def _():
        for copy in halo_copies():
            copy.wait_send()


def shards(peers, x_in, z_in, bc_in, wx, bx, wbc, bbc, dt_raw, dt_bias, decay, skip_d, gain, lengths):
    rows, chan = x_in.shape
    heads = dt_raw.shape[1]
    groups = bc_in.shape[2] // STATE
    width = wx.shape[0]
    chunks = chan // CHUNK
    pairs = chunks // 2
    bcw = 2 * groups * STATE
    vmem = pl.BlockSpec(memory_space=pltpu.VMEM)
    hbm = pl.BlockSpec(memory_space=pl.ANY)
    smem = pl.BlockSpec(memory_space=pltpu.SMEM)
    dma = pltpu.SemaphoreType.DMA
    return pl.pallas_call(
        functools.partial(kernel, peers),
        out_shape=jax.ShapeDtypeStruct((rows, chan), BF16),
        in_specs=[smem, hbm, hbm] + [vmem] * 10,
        out_specs=vmem,
        scratch_shapes=[
            pltpu.VMEM((rows, chan), BF16),
            pltpu.VMEM((rows, chan), BF16),
            pltpu.VMEM((rows, chan), BF16),
            pltpu.VMEM((rows, bcw), BF16),
            pltpu.VMEM((chunks, rows, CHUNK), BF16),
            pltpu.VMEM((chunks, STATE, CHUNK), BF16),
            pltpu.VMEM((width - 1, rows, TILE), F32),
            pltpu.VMEM((EDGE, chan), BF16),
            pltpu.VMEM((EDGE, bcw), BF16),
            pltpu.VMEM((EDGE, chan // FOLD), BF16),
            pltpu.VMEM((EDGE, chan // FOLD), BF16),
            pltpu.VMEM((chunks, 2 * heads, CHUNK), BF16),
            pltpu.VMEM((groups, rows, rows + STATE), BF16),
            pltpu.VMEM((groups, STATE, rows), BF16),
            pltpu.VMEM((rows, 2 * heads), BF16),
            pltpu.VMEM((rows, 2 * heads), BF16),
            pltpu.VMEM((16, 2 * heads), F32),
            pltpu.VMEM((16, 2 * heads), F32),
            pltpu.VMEM((chunks, 16, CHUNK), F32),
            pltpu.VMEM((pairs, STATE, CHUNK), BF16),
            pltpu.VMEM((pairs, STATE, CHUNK), F32),
            pltpu.VMEM((pairs, STATE, CHUNK), BF16),
            pltpu.VMEM((pairs, STATE, CHUNK), BF16),
            pltpu.VMEM((pairs, STATE, CHUNK), BF16),
            pltpu.VMEM((pairs, STATE, CHUNK), BF16),
            pltpu.VMEM((chunks, rows, CHUNK), F32),
            pltpu.VMEM((groups, rows, CHUNK), F32),
            dma((2,)),
            dma((2,)),
            dma((2,)),
            dma,
            dma,
            dma((pairs,)),
            dma((pairs,)),
            dma((pairs,)),
            dma((pairs,)),
            dma((pairs,)),
            dma((pairs,)),
        ],
        compiler_params=pltpu.CompilerParams(
            collective_id=0, has_side_effects=True, vmem_limit_bytes=63 * 1024 * 1024
        ),
        name="mixer",
    )(
        lengths,
        x_in,
        z_in,
        bc_in.reshape(rows, bcw),
        wx,
        bx.reshape(1, chan),
        wbc.reshape(width, bcw),
        bbc,
        dt_raw,
        dt_bias.reshape(1, heads),
        decay.reshape(1, heads),
        skip_d.reshape(1, heads),
        gain.reshape(1, chan),
    )


def solution(mesh):
    return jax.shard_map(
        functools.partial(shards, mesh.shape["seq"]),
        mesh=mesh,
        in_specs=(
            P(("groups", "seq"), "heads"),
            P(("groups", "seq"), "heads"),
            P(("groups", "seq"), None, "heads"),
            P(None, "heads"),
            P("heads"),
            P(None, None, "heads"),
            P(None, "heads"),
            P(("groups", "seq"), "heads"),
            P("heads"),
            P("heads"),
            P("heads"),
            P("heads"),
            P("groups"),
        ),
        out_specs=P(("groups", "seq"), "heads"),
        check_vma=False,
    )
```

```python
import functools

import jax
import jax.numpy as jnp
from jax import lax
from jax.experimental import pallas as pl
from jax.experimental.pallas import tpu as pltpu
from jax.sharding import PartitionSpec as P

HEAD_DIM = 64
STATE = 128
BLOCK = 128
TILE = 128
CHUNK = 256
EDGE = 16
LAG = 2
EARLY = 3
FOLD = 4
F32 = jnp.float32
BF16 = jnp.bfloat16
MESH = pl.DeviceIdType.MESH


def dot(a, b):
    return lax.dot_general(a, b, (((1,), (0,)), ((), ())), preferred_element_type=F32)


def silu(v):
    half = 0.5 * v
    return half + half * jnp.tanh(half)


def split(v):
    high = v.astype(BF16).astype(F32)
    return jnp.concatenate([high, v - high], axis=1)


def iota(shape, dim):
    return lax.broadcasted_iota(jnp.int32, shape, dim)


def spread(chunk, heads):
    per = CHUNK // HEAD_DIM
    row = iota((2 * heads, CHUNK), 0)
    col = iota((2 * heads, CHUNK), 1)
    head = jnp.where(row >= heads, row - heads, row)
    hit = head == chunk * per + lax.shift_right_logical(col, HEAD_DIM.bit_length() - 1)
    return jnp.where(hit, 1.0, 0.0).astype(BF16)


def conv_rows(values, weight, bias, flags, skip_rows):
    width = weight.shape[0]
    total = bias + values[skip_rows:] * weight[width - 1 : width]
    for d in range(1, width):
        moved = pltpu.roll(values, d, 0)[skip_rows:]
        total = total + moved * flags[d - 1] * weight[width - 1 - d : width - d]
    return silu(total).astype(BF16)


def kernel(
    peers,
    lengths,
    x_hbm,
    z_hbm,
    bc,
    wx,
    bx,
    wbc,
    bbc,
    dt,
    dtb,
    decay,
    skip,
    gain,
    out,
    xv,
    zv,
    xa,
    bca,
    xp,
    ent,
    flags,
    halo_x,
    halo_bc,
    fold_out,
    fold_in,
    spreads,
    mix,
    bt,
    grow,
    ggrow,
    vec,
    pvec,
    rows_x,
    s_out,
    s_own,
    s_in,
    e_in,
    e_out,
    t_out,
    gated,
    sumsq,
    local_sem,
    halo_send,
    halo_recv,
    vec_send,
    vec_recv,
    s_send,
    s_recv,
    e_send,
    e_recv,
    t_send,
    t_recv,
):
    rows, chan = x_hbm.shape
    heads = dt.shape[1]
    groups = bc.shape[1] // (2 * STATE)
    chunks = chan // CHUNK
    pairs = chunks // 2
    pairs_per = pairs // groups
    me = lax.axis_index("seq")
    inner = lax.rem(me, 2)
    outer = lax.div(me, 2)
    last_outer = peers // 2 - 1
    partner = me + 1 - 2 * inner

    load_x = pltpu.make_async_copy(x_hbm, xv, local_sem.at[0])
    load_z = pltpu.make_async_copy(z_hbm, zv, local_sem.at[1])
    load_x.start()
    load_z.start()

    barrier = pltpu.get_barrier_semaphore()
    for step in (-2, -1, 1, 2):
        there = me + step

        @pl.when((there >= 0) & (there < peers))
        def _():
            pl.semaphore_signal(barrier, inc=1, device_id={"seq": there}, device_id_type=MESH)

    present = jnp.minimum(me, 2) + jnp.minimum(peers - 1 - me, 2)

    start = me * rows
    ends = []
    total = jnp.int32(0)
    for j in range(lengths.shape[0]):
        total = total + lengths[j]
        ends.append(total)

    def seg_of(pos):
        count = jnp.zeros_like(pos)
        for end in ends:
            count = count + jnp.where(pos >= end, 1, 0)
        return jnp.where(pos >= 0, count, -1)

    square = (rows, rows)
    pos = iota(square, 0) + start
    seg_t = seg_of(pos)
    for d in range(1, wx.shape[0]):
        flags[d - 1] = jnp.where(seg_of(pos - d) == seg_t, 1.0, 0.0)
    seg_s = seg_of(iota(square, 1) + start)
    seg_last = seg_of(jnp.zeros(square, jnp.int32) + (start + rows - 1))
    seg_prev = seg_of(jnp.zeros(square, jnp.int32) + (start - 1))
    mask = jnp.where((seg_t == seg_s) & (iota(square, 0) >= iota(square, 1)), 1.0, 0.0)
    to_end = jnp.where(seg_t == seg_last, 1.0, 0.0)
    live = jnp.where(seg_t == seg_prev, 1.0, 0.0)

    raw = dt[...].astype(F32) + dtb[...]
    rate = jnp.maximum(raw, 0.0) + jnp.log(1.0 + jnp.exp(-jnp.abs(raw)))
    a = -rate * decay[...]
    tri = jnp.where(iota(square, 0) >= iota(square, 1), 1.0, 0.0).astype(BF16)
    cum = jnp.zeros_like(a)
    rest = a
    for _ in range(3):
        part = rest.astype(BF16)
        cum = cum + dot(tri, part)
        rest = rest - part.astype(F32)
    grow[...] = split(jnp.exp(cum)).astype(BF16)
    ggrow[...] = split(jnp.exp(-cum) * rate).astype(BF16)
    whole = jnp.exp(cum[rows - 1 : rows, :])
    carry = live[rows - 1 : rows, :heads] * whole
    which = iota(vec.shape, 0)
    vec[...] = jnp.where(
        which == 0, split(carry), jnp.where(which == 1, split(whole), jnp.where(which == 2, split(skip[...]), 0.0))
    )

    load_x.wait()
    run = chan // FOLD
    quarter = lax.shift_right_logical(iota((EDGE, run), 0), 2)
    folded = jnp.zeros((EDGE, run), F32)
    for m in range(FOLD):
        piece = xv[rows - EDGE :, m * run : (m + 1) * run].astype(F32)
        moved = pltpu.roll(piece, 4 * m + 4, 0) if m < FOLD - 1 else piece
        folded = jnp.where(quarter == m, moved, folded)
    fold_out[...] = folded.astype(BF16)

    pl.semaphore_wait(barrier, present)

    def halo_copies():
        there = jnp.minimum(me + 1, peers - 1)
        tail = pl.ds(rows - EDGE, EDGE)
        return [
            pltpu.make_async_remote_copy(
                fold_out, fold_in, halo_send.at[0], halo_recv.at[0], device_id={"seq": there}, device_id_type=MESH
            ),
            pltpu.make_async_remote_copy(
                bc.at[tail], halo_bc, halo_send.at[1], halo_recv.at[1], device_id={"seq": there}, device_id_type=MESH
            ),
        ]

    @pl.when(me < peers - 1)
    def _():
        for copy in halo_copies():
            copy.start()

    def vec_copy():
        return pltpu.make_async_remote_copy(
            vec, pvec, vec_send, vec_recv, device_id={"seq": partner}, device_id_type=MESH
        )

    vec_copy().start()

    bcols = groups * STATE

    def bc_params(tile):
        cols = slice((tile % groups) * TILE, (tile % groups + 1) * TILE)
        which = tile // groups
        return wbc[:, tile * TILE : (tile + 1) * TILE].astype(F32), bbc[which : which + 1, cols]

    bc_tiles = 2 * bcols // TILE
    for tile in range(bc_tiles):
        cols = slice(tile * TILE, (tile + 1) * TILE)
        weight, bias = bc_params(tile)
        bca[:, cols] = conv_rows(bc[:, cols].astype(F32), weight, bias, flags, 0)

    def x_params(cols):
        return wx[:, cols].astype(F32), bx[:, cols]

    def conv_tile(tile, _):
        cols = pl.ds(pl.multiple_of(tile * TILE, TILE), TILE)
        weight, bias = x_params(cols)
        xa[:, cols] = conv_rows(xv[:, cols].astype(F32), weight, bias, flags, 0)
        return 0

    early_tiles = EARLY * 2 * CHUNK // TILE
    lax.fori_loop(0, early_tiles, conv_tile, 0, unroll=2)

    @pl.when(me == 0)
    def _():
        fold_in[...] = jnp.zeros_like(fold_in)
        halo_bc[...] = jnp.zeros_like(halo_bc)

    @pl.when(me > 0)
    def _():
        for copy in halo_copies():
            copy.wait_recv()

    for m in range(FOLD):
        piece = fold_in[...].astype(F32)
        moved = pltpu.roll(piece, EDGE - 4 * m - 4, 0) if m < FOLD - 1 else piece
        halo_x[:, m * run : (m + 1) * run] = moved.astype(BF16)

    head_flags = [flags[d, :EDGE, :] for d in range(wx.shape[0] - 1)]
    for tile in range(bc_tiles):
        cols = slice(tile * TILE, (tile + 1) * TILE)
        weight, bias = bc_params(tile)
        values = jnp.concatenate([halo_bc[:, cols].astype(F32), bc[:EDGE, cols].astype(F32)], axis=0)
        bca[:EDGE, cols] = conv_rows(values, weight, bias, head_flags, EDGE)

    def conv_head(tile, _):
        cols = pl.ds(pl.multiple_of(tile * TILE, TILE), TILE)
        weight, bias = x_params(cols)
        values = jnp.concatenate([halo_x[:, cols].astype(F32), xv[:EDGE, cols].astype(F32)], axis=0)
        some = [flags[d, :EDGE, :] for d in range(wx.shape[0] - 1)]
        xa[:EDGE, cols] = conv_rows(values, weight, bias, some, EDGE)
        return 0

    lax.fori_loop(0, early_tiles, conv_head, 0, unroll=2)

    def conv_whole(tile, _):
        cols = pl.ds(pl.multiple_of(tile * TILE, TILE), TILE)
        weight, bias = x_params(cols)
        values = jnp.concatenate([halo_x[:, cols].astype(F32), xv[:, cols].astype(F32)], axis=0)
        xa[:, cols] = conv_rows(values, weight, bias, flags, EDGE)
        return 0

    for g in range(groups):
        bmat = bca[:, g * STATE : (g + 1) * STATE].astype(F32)
        cmat = bca[:, (groups + g) * STATE : (groups + g + 1) * STATE]
        bmat_t = jnp.transpose(bmat)
        scores = dot(cmat, bmat_t.astype(BF16))
        mix[g, :, :rows] = (scores * mask).astype(BF16)
        mix[g, :, rows:] = (cmat.astype(F32) * live).astype(BF16)
        bt[g] = jnp.transpose(bmat * to_end).astype(BF16)

    def state_of(c):
        ex = spread(c, heads)
        spreads[c] = ex
        cols = pl.ds(pl.multiple_of(c * CHUNK, CHUNK), CHUNK)
        scaled = (dot(ggrow[...], ex) * xa[:, cols].astype(F32)).astype(BF16)
        xp[c] = scaled
        rows_x[c] = dot(vec[...].astype(BF16), ex)
        return dot(bt[lax.div(c, chunks // groups)], scaled) * rows_x[c][1:2, :]

    def s_copy(j):
        return pltpu.make_async_remote_copy(
            s_out.at[j], s_in.at[j], s_send.at[j], s_recv.at[j], device_id={"seq": partner}, device_id_type=MESH
        )

    def e_copy(j):
        there = jnp.minimum(me + 2, peers - 1)
        return pltpu.make_async_remote_copy(
            e_out.at[j], e_in.at[j], e_send.at[j], e_recv.at[j], device_id={"seq": there}, device_id_type=MESH
        )

    def t_copy(j, c):
        return pltpu.make_async_remote_copy(
            t_out.at[j], ent.at[c], t_send.at[j], t_recv.at[j], device_id={"seq": partner}, device_id_type=MESH
        )

    hold = jnp.maximum(pairs - 1 - 2 * outer, 0)
    behind = jnp.minimum(hold + LAG, pairs)

    def advance(j):
        c = 2 * j + inner
        s_copy(j).wait_recv()

        @pl.when(outer > 0)
        def _():
            e_copy(j).wait_recv()

        mine = s_own[j]
        other = s_in[j].astype(F32)
        c_mine = rows_x[c][0:1, :]
        c_other = dot(pvec[...].astype(BF16), spreads[c])[0:1, :]
        first = jnp.broadcast_to(inner, mine.shape) == 0
        row_first = jnp.broadcast_to(inner, c_mine.shape) == 0
        e = e_in[j].astype(F32)
        between = jnp.where(row_first, c_mine, c_other) * e + jnp.where(first, mine, other)
        after = jnp.where(row_first, c_other, c_mine) * between + jnp.where(first, other, mine)
        e_out[j] = after.astype(BF16)

        @pl.when(outer < last_outer)
        def _():
            e_copy(j).start()

        t_out[j] = jnp.where(first, between, e).astype(BF16)

        @pl.when(j == hold)
        def _():
            def release(k, _):
                t_copy(k, 2 * k + inner).start()
                return 0

            lax.fori_loop(0, hold + 1, release, 0)

        @pl.when(j > hold)
        def _():
            t_copy(j, c).start()

        ent[c] = jnp.where(first, e, between).astype(BF16)

    @pl.when(outer == 0)
    def _():
        e_in[...] = jnp.zeros_like(e_in)

    vec_copy().wait_recv()
    sumsq[...] = jnp.zeros_like(sumsq)
    ahead = jnp.where(outer == 0, pairs - LAG, 0)

    def states(j, _):
        @pl.when(j >= EARLY)
        def _():
            per = 2 * CHUNK // TILE
            for k in range(per):
                conv_whole(j * per + k, 0)

        s_out[j] = state_of(2 * j + 1 - inner).astype(BF16)
        s_copy(j).start()
        s_own[j] = state_of(2 * j + inner)

        @pl.when((outer == 0) & (j >= LAG))
        def _():
            advance(j - LAG)

        return 0

    lax.fori_loop(0, pairs, states, 0)
    load_z.wait()

    def finish_chunk(c):
        g = lax.div(c, chunks // groups)
        cols = pl.ds(pl.multiple_of(c * CHUNK, CHUNK), CHUNK)
        right = jnp.concatenate([xp[c], ent[c]], axis=0)
        y = dot(mix[g], right) * dot(grow[...], spreads[c])
        y = y + rows_x[c][2:3, :] * xa[:, cols].astype(F32)
        v = y.astype(BF16).astype(F32) * silu(zv[:, cols].astype(F32))
        gated[c] = v
        sumsq[g] = sumsq[g] + v * v

    def finish_pair(j):
        t_copy(j, 2 * j + 1 - inner).wait_recv()
        finish_chunk(2 * j)
        finish_chunk(2 * j + 1)

    def norm_group(g):
        size = chan // groups
        mean = jnp.sum(sumsq[g], axis=1, keepdims=True) * (1.0 / size)
        scale = lax.rsqrt(mean + 1e-05)

        def one(k, _):
            c = g * (chunks // groups) + k
            cols = pl.ds(pl.multiple_of(c * CHUNK, CHUNK), CHUNK)
            out[:, cols] = (gated[c] * scale * gain[:, cols]).astype(BF16)
            return 0

        lax.fori_loop(0, chunks // groups, one, 0, unroll=2)

    def finish_and_norm(j):
        finish_pair(j)

        @pl.when(lax.rem(j + 1, pairs_per) == 0)
        def _():
            norm_group(lax.div(j, pairs_per))

    def steady(j, _):
        @pl.when((j >= ahead) & (j < pairs))
        def _():
            advance(j)

        @pl.when(j >= behind)
        def _():
            finish_and_norm(j - behind)

        return 0

    lax.fori_loop(0, pairs + behind, steady, 0)

    def drain(j, _):
        s_copy(j).wait_send()
        t_copy(j, 2 * j + inner).wait_send()

        @pl.when(outer < last_outer)
        def _():
            e_copy(j).wait_send()

        return 0

    lax.fori_loop(0, pairs, drain, 0)
    vec_copy().wait_send()

    @pl.when(me < peers - 1)
    def _():
        for copy in halo_copies():
            copy.wait_send()


def shards(peers, x_in, z_in, bc_in, wx, bx, wbc, bbc, dt_raw, dt_bias, decay, skip_d, gain, lengths):
    rows, chan = x_in.shape
    heads = dt_raw.shape[1]
    groups = bc_in.shape[2] // STATE
    width = wx.shape[0]
    chunks = chan // CHUNK
    pairs = chunks // 2
    bcw = 2 * groups * STATE
    vmem = pl.BlockSpec(memory_space=pltpu.VMEM)
    hbm = pl.BlockSpec(memory_space=pltpu.HBM)
    smem = pl.BlockSpec(memory_space=pltpu.SMEM)
    dma = pltpu.SemaphoreType.DMA
    return pl.pallas_call(
        functools.partial(kernel, peers),
        out_shape=jax.ShapeDtypeStruct((rows, chan), BF16),
        in_specs=[smem, hbm, hbm] + [vmem] * 10,
        out_specs=vmem,
        scratch_shapes=[
            pltpu.VMEM((rows, chan), BF16),
            pltpu.VMEM((rows, chan), BF16),
            pltpu.VMEM((rows, chan), BF16),
            pltpu.VMEM((rows, bcw), BF16),
            pltpu.VMEM((chunks, rows, CHUNK), BF16),
            pltpu.VMEM((chunks, STATE, CHUNK), BF16),
            pltpu.VMEM((width - 1, rows, TILE), F32),
            pltpu.VMEM((EDGE, chan), BF16),
            pltpu.VMEM((EDGE, bcw), BF16),
            pltpu.VMEM((EDGE, chan // FOLD), BF16),
            pltpu.VMEM((EDGE, chan // FOLD), BF16),
            pltpu.VMEM((chunks, 2 * heads, CHUNK), BF16),
            pltpu.VMEM((groups, rows, rows + STATE), BF16),
            pltpu.VMEM((groups, STATE, rows), BF16),
            pltpu.VMEM((rows, 2 * heads), BF16),
            pltpu.VMEM((rows, 2 * heads), BF16),
            pltpu.VMEM((16, 2 * heads), F32),
            pltpu.VMEM((16, 2 * heads), F32),
            pltpu.VMEM((chunks, 16, CHUNK), F32),
            pltpu.VMEM((pairs, STATE, CHUNK), BF16),
            pltpu.VMEM((pairs, STATE, CHUNK), F32),
            pltpu.VMEM((pairs, STATE, CHUNK), BF16),
            pltpu.VMEM((pairs, STATE, CHUNK), BF16),
            pltpu.VMEM((pairs, STATE, CHUNK), BF16),
            pltpu.VMEM((pairs, STATE, CHUNK), BF16),
            pltpu.VMEM((chunks, rows, CHUNK), F32),
            pltpu.VMEM((groups, rows, CHUNK), F32),
            dma((2,)),
            dma((2,)),
            dma((2,)),
            dma,
            dma,
            dma((pairs,)),
            dma((pairs,)),
            dma((pairs,)),
            dma((pairs,)),
            dma((pairs,)),
            dma((pairs,)),
        ],
        compiler_params=pltpu.CompilerParams(
            collective_id=0, has_side_effects=True, vmem_limit_bytes=52 * 1024 * 1024
        ),
        name="mixer",
    )(
        lengths,
        x_in,
        z_in,
        bc_in.reshape(rows, bcw),
        wx,
        bx.reshape(1, chan),
        wbc.reshape(width, bcw),
        bbc,
        dt_raw,
        dt_bias.reshape(1, heads),
        decay.reshape(1, heads),
        skip_d.reshape(1, heads),
        gain.reshape(1, chan),
    )


def solution(mesh):
    return jax.shard_map(
        functools.partial(shards, mesh.shape["seq"]),
        mesh=mesh,
        in_specs=(
            P(("groups", "seq"), "heads"),
            P(("groups", "seq"), "heads"),
            P(("groups", "seq"), None, "heads"),
            P(None, "heads"),
            P("heads"),
            P(None, None, "heads"),
            P(None, "heads"),
            P(("groups", "seq"), "heads"),
            P("heads"),
            P("heads"),
            P("heads"),
            P("heads"),
            P("groups"),
        ),
        out_specs=P(("groups", "seq"), "heads"),
        check_vma=False,
    )
```

```python
import functools

import jax
import jax.numpy as jnp
from jax import lax
from jax.experimental import pallas as pl
from jax.experimental.pallas import tpu as pltpu
from jax.sharding import PartitionSpec as P

HEAD_DIM = 64
STATE = 128
BLOCK = 128
TILE = 128
CHUNK = 256
EDGE = 16
LAG = 2
EARLY = 3
FOLD = 4
F32 = jnp.float32
BF16 = jnp.bfloat16
MESH = pl.DeviceIdType.MESH


def dot(a, b):
    return lax.dot_general(a, b, (((1,), (0,)), ((), ())), preferred_element_type=F32)


def silu(v):
    half = 0.5 * v
    return half + half * jnp.tanh(half)


def split(v):
    high = v.astype(BF16).astype(F32)
    return jnp.concatenate([high, v - high], axis=1)


def iota(shape, dim):
    return lax.broadcasted_iota(jnp.int32, shape, dim)


def spread(chunk, heads):
    per = CHUNK // HEAD_DIM
    row = iota((2 * heads, CHUNK), 0)
    col = iota((2 * heads, CHUNK), 1)
    head = jnp.where(row >= heads, row - heads, row)
    hit = head == chunk * per + lax.shift_right_logical(col, HEAD_DIM.bit_length() - 1)
    return jnp.where(hit, 1.0, 0.0).astype(BF16)


def conv_rows(values, weight, bias, flags, skip_rows):
    width = weight.shape[0]
    total = bias + values[skip_rows:] * weight[width - 1 : width]
    for d in range(1, width):
        moved = pltpu.roll(values, d, 0)[skip_rows:]
        total = total + moved * flags[d - 1] * weight[width - 1 - d : width - d]
    return silu(total).astype(BF16)


def kernel(
    peers,
    lengths,
    x_hbm,
    z_hbm,
    bc,
    wx,
    bx,
    wbc,
    bbc,
    dt,
    dtb,
    decay,
    skip,
    gain,
    out,
    xv,
    zv,
    xa,
    bca,
    xp,
    ent,
    flags,
    halo_x,
    halo_bc,
    fold_out,
    fold_in,
    spreads,
    mix,
    bt,
    grow,
    ggrow,
    vec,
    pvec,
    rows_x,
    s_out,
    s_own,
    s_in,
    e_in,
    e_out,
    t_out,
    gated,
    sumsq,
    local_sem,
    halo_send,
    halo_recv,
    vec_send,
    vec_recv,
    s_send,
    s_recv,
    e_send,
    e_recv,
    t_send,
    t_recv,
):
    rows, chan = x_hbm.shape
    heads = dt.shape[1]
    groups = bc.shape[1] // (2 * STATE)
    chunks = chan // CHUNK
    pairs = chunks // 2
    pairs_per = pairs // groups
    me = lax.axis_index("seq")
    inner = lax.rem(me, 2)
    outer = lax.div(me, 2)
    last_outer = peers // 2 - 1
    partner = me + 1 - 2 * inner

    load_x = pltpu.make_async_copy(x_hbm, xv, local_sem.at[0])
    load_z = pltpu.make_async_copy(z_hbm, zv, local_sem.at[1])
    load_x.start()
    load_z.start()

    barrier = pltpu.get_barrier_semaphore()
    for step in (-2, -1, 1, 2):
        there = me + step

        @pl.when((there >= 0) & (there < peers))
        def _():
            pl.semaphore_signal(barrier, inc=1, device_id={"seq": there}, device_id_type=MESH)

    present = jnp.minimum(me, 2) + jnp.minimum(peers - 1 - me, 2)

    start = me * rows
    ends = []
    total = jnp.int32(0)
    for j in range(lengths.shape[0]):
        total = total + lengths[j]
        ends.append(total)

    def seg_of(pos):
        count = jnp.zeros_like(pos)
        for end in ends:
            count = count + jnp.where(pos >= end, 1, 0)
        return jnp.where(pos >= 0, count, -1)

    square = (rows, rows)
    pos = iota(square, 0) + start
    seg_t = seg_of(pos)
    for d in range(1, wx.shape[0]):
        flags[d - 1] = jnp.where(seg_of(pos - d) == seg_t, 1.0, 0.0)
    seg_s = seg_of(iota(square, 1) + start)
    seg_last = seg_of(jnp.zeros(square, jnp.int32) + (start + rows - 1))
    seg_prev = seg_of(jnp.zeros(square, jnp.int32) + (start - 1))
    mask = jnp.where((seg_t == seg_s) & (iota(square, 0) >= iota(square, 1)), 1.0, 0.0)
    to_end = jnp.where(seg_t == seg_last, 1.0, 0.0)
    live = jnp.where(seg_t == seg_prev, 1.0, 0.0)

    raw = dt[...].astype(F32) + dtb[...]
    rate = jnp.maximum(raw, 0.0) + jnp.log(1.0 + jnp.exp(-jnp.abs(raw)))
    a = -rate * decay[...]
    tri = jnp.where(iota(square, 0) >= iota(square, 1), 1.0, 0.0).astype(BF16)
    cum = jnp.zeros_like(a)
    rest = a
    for _ in range(3):
        part = rest.astype(BF16)
        cum = cum + dot(tri, part)
        rest = rest - part.astype(F32)
    grow[...] = split(jnp.exp(cum)).astype(BF16)
    ggrow[...] = split(jnp.exp(-cum) * rate).astype(BF16)
    whole = jnp.exp(cum[rows - 1 : rows, :])
    carry = live[rows - 1 : rows, :heads] * whole
    which = iota(vec.shape, 0)
    vec[...] = jnp.where(
        which == 0, split(carry), jnp.where(which == 1, split(whole), jnp.where(which == 2, split(skip[...]), 0.0))
    )

    load_x.wait()
    run = chan // FOLD
    quarter = lax.shift_right_logical(iota((EDGE, run), 0), 2)
    folded = jnp.zeros((EDGE, run), F32)
    for m in range(FOLD):
        piece = xv[rows - EDGE :, m * run : (m + 1) * run].astype(F32)
        moved = pltpu.roll(piece, 4 * m + 4, 0) if m < FOLD - 1 else piece
        folded = jnp.where(quarter == m, moved, folded)
    fold_out[...] = folded.astype(BF16)

    pl.semaphore_wait(barrier, present)

    def halo_copies():
        there = jnp.minimum(me + 1, peers - 1)
        tail = pl.ds(rows - EDGE, EDGE)
        return [
            pltpu.make_async_remote_copy(
                fold_out, fold_in, halo_send.at[0], halo_recv.at[0], device_id={"seq": there}, device_id_type=MESH
            ),
            pltpu.make_async_remote_copy(
                bc.at[tail], halo_bc, halo_send.at[1], halo_recv.at[1], device_id={"seq": there}, device_id_type=MESH
            ),
        ]

    @pl.when(me < peers - 1)
    def _():
        for copy in halo_copies():
            copy.start()

    def vec_copy():
        return pltpu.make_async_remote_copy(
            vec, pvec, vec_send, vec_recv, device_id={"seq": partner}, device_id_type=MESH
        )

    vec_copy().start()

    bcols = groups * STATE

    def bc_params(tile):
        cols = slice((tile % groups) * TILE, (tile % groups + 1) * TILE)
        which = tile // groups
        return wbc[...].astype(F32)[:, which, cols], bbc[which : which + 1, cols]

    bc_tiles = 2 * bcols // TILE
    for tile in range(bc_tiles):
        cols = slice(tile * TILE, (tile + 1) * TILE)
        weight, bias = bc_params(tile)
        bca[:, cols] = conv_rows(bc[:, cols].astype(F32), weight, bias, flags, 0)

    def x_params(cols):
        return wx[:, cols].astype(F32), bx[:, cols]

    def conv_tile(tile, _):
        cols = pl.ds(pl.multiple_of(tile * TILE, TILE), TILE)
        weight, bias = x_params(cols)
        xa[:, cols] = conv_rows(xv[:, cols].astype(F32), weight, bias, flags, 0)
        return 0

    early_tiles = EARLY * 2 * CHUNK // TILE
    lax.fori_loop(0, early_tiles, conv_tile, 0, unroll=2)

    @pl.when(me == 0)
    def _():
        fold_in[...] = jnp.zeros_like(fold_in)
        halo_bc[...] = jnp.zeros_like(halo_bc)

    @pl.when(me > 0)
    def _():
        for copy in halo_copies():
            copy.wait_recv()

    for m in range(FOLD):
        piece = fold_in[...].astype(F32)
        moved = pltpu.roll(piece, EDGE - 4 * m - 4, 0) if m < FOLD - 1 else piece
        halo_x[:, m * run : (m + 1) * run] = moved.astype(BF16)

    head_flags = [flags[d, :EDGE, :] for d in range(wx.shape[0] - 1)]
    for tile in range(bc_tiles):
        cols = slice(tile * TILE, (tile + 1) * TILE)
        weight, bias = bc_params(tile)
        values = jnp.concatenate([halo_bc[:, cols].astype(F32), bc[:EDGE, cols].astype(F32)], axis=0)
        bca[:EDGE, cols] = conv_rows(values, weight, bias, head_flags, EDGE)

    def conv_head(tile, _):
        cols = pl.ds(pl.multiple_of(tile * TILE, TILE), TILE)
        weight, bias = x_params(cols)
        values = jnp.concatenate([halo_x[:, cols].astype(F32), xv[:EDGE, cols].astype(F32)], axis=0)
        some = [flags[d, :EDGE, :] for d in range(wx.shape[0] - 1)]
        xa[:EDGE, cols] = conv_rows(values, weight, bias, some, EDGE)
        return 0

    lax.fori_loop(0, early_tiles, conv_head, 0, unroll=2)

    def conv_whole(tile, _):
        cols = pl.ds(pl.multiple_of(tile * TILE, TILE), TILE)
        weight, bias = x_params(cols)
        values = jnp.concatenate([halo_x[:, cols].astype(F32), xv[:, cols].astype(F32)], axis=0)
        xa[:, cols] = conv_rows(values, weight, bias, flags, EDGE)
        return 0

    for g in range(groups):
        bmat = bca[:, g * STATE : (g + 1) * STATE].astype(F32)
        cmat = bca[:, (groups + g) * STATE : (groups + g + 1) * STATE]
        bmat_t = jnp.transpose(bmat)
        scores = dot(cmat, bmat_t.astype(BF16))
        mix[g, :, :rows] = (scores * mask).astype(BF16)
        mix[g, :, rows:] = (cmat.astype(F32) * live).astype(BF16)
        bt[g] = jnp.transpose(bmat * to_end).astype(BF16)

    def state_of(c):
        ex = spread(c, heads)
        spreads[c] = ex
        cols = pl.ds(pl.multiple_of(c * CHUNK, CHUNK), CHUNK)
        scaled = (dot(ggrow[...], ex) * xa[:, cols].astype(F32)).astype(BF16)
        xp[c] = scaled
        rows_x[c] = dot(vec[...].astype(BF16), ex)
        return dot(bt[lax.div(c, chunks // groups)], scaled) * rows_x[c][1:2, :]

    def s_copy(j):
        return pltpu.make_async_remote_copy(
            s_out.at[j], s_in.at[j], s_send.at[j], s_recv.at[j], device_id={"seq": partner}, device_id_type=MESH
        )

    def e_copy(j):
        there = jnp.minimum(me + 2, peers - 1)
        return pltpu.make_async_remote_copy(
            e_out.at[j], e_in.at[j], e_send.at[j], e_recv.at[j], device_id={"seq": there}, device_id_type=MESH
        )

    def t_copy(j, c):
        return pltpu.make_async_remote_copy(
            t_out.at[j], ent.at[c], t_send.at[j], t_recv.at[j], device_id={"seq": partner}, device_id_type=MESH
        )

    hold = jnp.maximum(pairs - 1 - 2 * outer, 0)
    behind = jnp.minimum(hold + LAG, pairs)

    def advance(j):
        c = 2 * j + inner
        s_copy(j).wait_recv()

        @pl.when(outer > 0)
        def _():
            e_copy(j).wait_recv()

        mine = s_own[j]
        other = s_in[j].astype(F32)
        c_mine = rows_x[c][0:1, :]
        c_other = dot(pvec[...].astype(BF16), spreads[c])[0:1, :]
        first = jnp.broadcast_to(inner, mine.shape) == 0
        row_first = jnp.broadcast_to(inner, c_mine.shape) == 0
        e = e_in[j].astype(F32)
        between = jnp.where(row_first, c_mine, c_other) * e + jnp.where(first, mine, other)
        after = jnp.where(row_first, c_other, c_mine) * between + jnp.where(first, other, mine)
        e_out[j] = after.astype(BF16)

        @pl.when(outer < last_outer)
        def _():
            e_copy(j).start()

        t_out[j] = jnp.where(first, between, e).astype(BF16)

        @pl.when(j == hold)
        def _():
            def release(k, _):
                t_copy(k, 2 * k + inner).start()
                return 0

            lax.fori_loop(0, hold + 1, release, 0)

        @pl.when(j > hold)
        def _():
            t_copy(j, c).start()

        ent[c] = jnp.where(first, e, between).astype(BF16)

    @pl.when(outer == 0)
    def _():
        e_in[...] = jnp.zeros_like(e_in)

    vec_copy().wait_recv()
    sumsq[...] = jnp.zeros_like(sumsq)
    ahead = jnp.where(outer == 0, pairs - LAG, 0)

    def states(j, _):
        @pl.when(j >= EARLY)
        def _():
            per = 2 * CHUNK // TILE
            for k in range(per):
                conv_whole(j * per + k, 0)

        s_out[j] = state_of(2 * j + 1 - inner).astype(BF16)
        s_copy(j).start()
        s_own[j] = state_of(2 * j + inner)

        @pl.when((outer == 0) & (j >= LAG))
        def _():
            advance(j - LAG)

        return 0

    lax.fori_loop(0, pairs, states, 0)
    load_z.wait()

    def finish_chunk(c):
        g = lax.div(c, chunks // groups)
        cols = pl.ds(pl.multiple_of(c * CHUNK, CHUNK), CHUNK)
        right = jnp.concatenate([xp[c], ent[c]], axis=0)
        y = dot(mix[g], right) * dot(grow[...], spreads[c])
        y = y + rows_x[c][2:3, :] * xa[:, cols].astype(F32)
        v = y.astype(BF16).astype(F32) * silu(zv[:, cols].astype(F32))
        gated[c] = v
        sumsq[g] = sumsq[g] + v * v

    def finish_pair(j):
        t_copy(j, 2 * j + 1 - inner).wait_recv()
        finish_chunk(2 * j)
        finish_chunk(2 * j + 1)

    def norm_group(g):
        size = chan // groups
        mean = jnp.sum(sumsq[g], axis=1, keepdims=True) * (1.0 / size)
        scale = lax.rsqrt(mean + 1e-05)

        def one(k, _):
            c = g * (chunks // groups) + k
            cols = pl.ds(pl.multiple_of(c * CHUNK, CHUNK), CHUNK)
            out[:, cols] = (gated[c] * scale * gain[:, cols]).astype(BF16)
            return 0

        lax.fori_loop(0, chunks // groups, one, 0, unroll=2)

    def finish_and_norm(j):
        finish_pair(j)

        @pl.when(lax.rem(j + 1, pairs_per) == 0)
        def _():
            norm_group(lax.div(j, pairs_per))

    def steady(j, _):
        @pl.when((j >= ahead) & (j < pairs))
        def _():
            advance(j)

        @pl.when(j >= behind)
        def _():
            finish_and_norm(j - behind)

        return 0

    lax.fori_loop(0, pairs + behind, steady, 0)

    def drain(j, _):
        s_copy(j).wait_send()
        t_copy(j, 2 * j + inner).wait_send()

        @pl.when(outer < last_outer)
        def _():
            e_copy(j).wait_send()

        return 0

    lax.fori_loop(0, pairs, drain, 0)
    vec_copy().wait_send()

    @pl.when(me < peers - 1)
    def _():
        for copy in halo_copies():
            copy.wait_send()


def shards(peers, x_in, z_in, bc_in, wx, bx, wbc, bbc, dt_raw, dt_bias, decay, skip_d, gain, lengths):
    rows, chan = x_in.shape
    heads = dt_raw.shape[1]
    groups = bc_in.shape[2] // STATE
    width = wx.shape[0]
    chunks = chan // CHUNK
    pairs = chunks // 2
    bcw = 2 * groups * STATE
    vmem = pl.BlockSpec(memory_space=pltpu.VMEM)
    hbm = pl.BlockSpec(memory_space=pltpu.HBM)
    smem = pl.BlockSpec(memory_space=pltpu.SMEM)
    dma = pltpu.SemaphoreType.DMA
    return pl.pallas_call(
        functools.partial(kernel, peers),
        out_shape=jax.ShapeDtypeStruct((rows, chan), BF16),
        in_specs=[smem, hbm, hbm] + [vmem] * 10,
        out_specs=vmem,
        scratch_shapes=[
            pltpu.VMEM((rows, chan), BF16),
            pltpu.VMEM((rows, chan), BF16),
            pltpu.VMEM((rows, chan), BF16),
            pltpu.VMEM((rows, bcw), BF16),
            pltpu.VMEM((chunks, rows, CHUNK), BF16),
            pltpu.VMEM((chunks, STATE, CHUNK), BF16),
            pltpu.VMEM((width - 1, rows, TILE), F32),
            pltpu.VMEM((EDGE, chan), BF16),
            pltpu.VMEM((EDGE, bcw), BF16),
            pltpu.VMEM((EDGE, chan // FOLD), BF16),
            pltpu.VMEM((EDGE, chan // FOLD), BF16),
            pltpu.VMEM((chunks, 2 * heads, CHUNK), BF16),
            pltpu.VMEM((groups, rows, rows + STATE), BF16),
            pltpu.VMEM((groups, STATE, rows), BF16),
            pltpu.VMEM((rows, 2 * heads), BF16),
            pltpu.VMEM((rows, 2 * heads), BF16),
            pltpu.VMEM((16, 2 * heads), F32),
            pltpu.VMEM((16, 2 * heads), F32),
            pltpu.VMEM((chunks, 16, CHUNK), F32),
            pltpu.VMEM((pairs, STATE, CHUNK), BF16),
            pltpu.VMEM((pairs, STATE, CHUNK), F32),
            pltpu.VMEM((pairs, STATE, CHUNK), BF16),
            pltpu.VMEM((pairs, STATE, CHUNK), BF16),
            pltpu.VMEM((pairs, STATE, CHUNK), BF16),
            pltpu.VMEM((pairs, STATE, CHUNK), BF16),
            pltpu.VMEM((chunks, rows, CHUNK), F32),
            pltpu.VMEM((groups, rows, CHUNK), F32),
            dma((2,)),
            dma((2,)),
            dma((2,)),
            dma,
            dma,
            dma((pairs,)),
            dma((pairs,)),
            dma((pairs,)),
            dma((pairs,)),
            dma((pairs,)),
            dma((pairs,)),
        ],
        compiler_params=pltpu.CompilerParams(
            collective_id=0, has_side_effects=True, vmem_limit_bytes=52 * 1024 * 1024
        ),
        name="mixer",
    )(
        lengths,
        x_in,
        z_in,
        bc_in.reshape(rows, bcw),
        wx,
        bx.reshape(1, chan),
        wbc,
        bbc,
        dt_raw,
        dt_bias.reshape(1, heads),
        decay.reshape(1, heads),
        skip_d.reshape(1, heads),
        gain.reshape(1, chan),
    )


def solution(mesh):
    return jax.shard_map(
        functools.partial(shards, mesh.shape["seq"]),
        mesh=mesh,
        in_specs=(
            P(("groups", "seq"), "heads"),
            P(("groups", "seq"), "heads"),
            P(("groups", "seq"), None, "heads"),
            P(None, "heads"),
            P("heads"),
            P(None, None, "heads"),
            P(None, "heads"),
            P(("groups", "seq"), "heads"),
            P("heads"),
            P("heads"),
            P("heads"),
            P("heads"),
            P("groups"),
        ),
        out_specs=P(("groups", "seq"), "heads"),
        check_vma=False,
    )
```
